32 devices in a mesh: groups: 2 (over y), row: 2 (over x), col: 4 (over z), tensor: 2 (over core).
Axes of the slice: x: 2, y: 2, z: 4, core: 2. Of those that a mesh axis runs over, the one named last changes fastest.
Arguments:
- activations: bfloat16 [2048, 14336], P(('groups', 'row', 'col'), 'tensor'), parts along dimension 0, may hold values from -320 to 320
- out_grads: bfloat16 [2048, 4096], P(('groups', 'row', 'col'), 'tensor'), parts along dimension 0, may hold values from -320 to 320
- proj_in: bfloat16 [14336, 64], P('tensor'), may hold values from -0.046875 to 0.046875
- proj_out: bfloat16 [4096, 64], P('tensor'), may hold values from -0.09375 to 0.09375
- lengths: int32 [32], P(('groups', 'row', 'col')), parts along dimension 0, may hold values from 16 to 64
- val_sketches: bfloat16 [16384, 4096], P(('groups', 'col', 'tensor'), 'row'), parts along dimension 0, may hold values from -190 to 190
Outputs:
- scores: float32 [32, 8192], P(('groups', 'row'), ('col', 'tensor')), parts along dimension 0
The draws below stay inside these ranges and needn't reach their ends.
There are 2 independent parts, one for each index of `groups`. The reference program is written for one: setup_inputs(seed, part) draws one part's arguments, and reference() takes and returns one part's arrays. A program takes and returns all parts, laid end to end along the dimension named above; an argument that names none is the same for every part. Nothing has to cross between parts.
All inputs are finite; a program needn't handle non-finite values.
Results may differ from the reference program's by a relative error of at most 0.005.
Values may be sent and summed in bfloat16 or wider, within the bound.
A program may use at most 64 MiB of HBM per device.

```python
import jax
import jax.numpy as jnp
from jax import lax

D = 4096
FF = 14336
RANK = 64
SEQ = 64
SK = 4096
NT = 16
NV = 8192
TOKS = 1024


def spread_scales(key, rows, cols, top):
    first, second = jax.random.split(key)
    row_scale = jnp.exp(jax.random.uniform(first, (rows, 1), jnp.float32, 0.0, jnp.log(top)))
    col_scale = jnp.exp(jax.random.uniform(second, (1, cols), jnp.float32, 0.0, jnp.log(top)))
    return row_scale * col_scale


def draw_activations(key, part):
    key = jax.random.fold_in(key, 11)
    base_key, scale_key = jax.random.split(key, 2)
    base = jnp.clip(jax.random.normal(base_key, (TOKS, FF), jnp.float32), -6.0, 6.0)
    scales = spread_scales(scale_key, TOKS, FF, 10.0)
    return (0.3 * base * scales).astype(jnp.bfloat16)


def draw_out_grads(key, part):
    key = jax.random.fold_in(key, 12)
    base_key, scale_key = jax.random.split(key, 2)
    base = jnp.clip(jax.random.normal(base_key, (TOKS, D), jnp.float32), -6.0, 6.0)
    scales = spread_scales(scale_key, TOKS, D, 10.0)
    return (0.3 * base * scales).astype(jnp.bfloat16)


def draw_val_sketches(key, part):
    key = jax.random.fold_in(key, 13)
    base_key, scale_key = jax.random.split(key, 2)
    ramp = jnp.sqrt(1.0 + 2.0 * jnp.arange(SK, dtype=jnp.float32)[None, :] / (SK - 1))
    base = jnp.clip(jax.random.normal(base_key, (NV, SK), jnp.float32), -6.0, 6.0)
    scales = spread_scales(scale_key, NV, SK, 10.0)
    return (0.1 * base * scales * ramp).astype(jnp.bfloat16)


def plant(entries, stream_key, low, high):
    longest = entries.shape.index(max(entries.shape))
    spots = []
    for shift in (0, 1):
        where = [jax.random.randint(jax.random.fold_in(stream_key, axis), (), 0, length) for axis, length in enumerate(entries.shape)]
        where[longest] = (where[longest] + shift) % entries.shape[longest]
        spots.append(tuple(where))
    return entries.at[spots[0]].set(low).at[spots[1]].set(high)


def shard_levels(key, shape, shards, smallest, top_value):
    def one(dim, shards_of):
        steps = jax.random.uniform(jax.random.fold_in(jax.random.fold_in(key, 6), dim), (shards_of,), jnp.float32, smallest / len(shards), top_value / len(shards))
        return jnp.repeat(jnp.exp(steps), shape[dim] // shards_of).reshape((-1,) + (1,) * (len(shape) - dim - 1))

    level = one(*shards[0])
    for cut in shards[1:]:
        level = level * one(*cut)
    return level


def scatter_about(rng, extent, width, reach, cuts=(), held_as=jnp.bfloat16):
    entries = jax.random.normal(rng, extent, jnp.float32) * width
    if len(cuts) > 0:
        entries = shard_levels(rng, extent, cuts, -0.22, 0.18) * entries
    return jnp.clip(entries, min=-reach, max=reach).astype(held_as)


def setup_inputs(seed: int = 0, part: int = 0) -> dict:
    keys = jax.random.split(jax.random.key(seed), 7)
    part_splits = jax.random.split(jax.random.fold_in(keys[6], part), 7)
    return {
        "activations": draw_activations(jax.random.fold_in(jax.random.fold_in(keys[6], part), 71), part),
        "out_grads": draw_out_grads(jax.random.fold_in(jax.random.fold_in(keys[6], part), 71), part),
        "proj_in": scatter_about(keys[2], (FF, RANK), FF ** -0.5, 0.046875, ((0, 2),)),
        "proj_out": scatter_about(keys[3], (D, RANK), D ** -0.5, 0.09375, ((0, 2),)),
        "lengths": plant(jax.random.randint(part_splits[4], (NT,), SEQ // 4, SEQ + 1), jax.random.fold_in(part_splits[4], 1), SEQ // 4, SEQ).astype(jnp.int32),
        "val_sketches": draw_val_sketches(jax.random.fold_in(jax.random.fold_in(keys[6], part), 71), part),
    }


def reference(activations, out_grads, proj_in, proj_out, lengths, val_sketches):
    examples = lengths.shape[0]
    seq = activations.shape[0] // examples
    rank = proj_in.shape[1]
    weight_in = proj_in.astype(jnp.float32)
    weight_out = proj_out.astype(jnp.float32)
    acts = activations.reshape(examples, seq, activations.shape[1])
    grads = out_grads.reshape(examples, seq, out_grads.shape[1])

    def one_example(items):
        rows_in, rows_out, length = items
        inner = jnp.dot(rows_in.astype(jnp.float32), weight_in, preferred_element_type=jnp.float32)
        outer = jnp.dot(rows_out.astype(jnp.float32), weight_out, preferred_element_type=jnp.float32)
        coded = jnp.concatenate([inner, outer], axis=1).astype(jnp.bfloat16)
        coded = lax.optimization_barrier(coded).astype(jnp.float32)
        left = coded[:, :rank]
        kept = (jnp.arange(seq, dtype=jnp.int32) < length).astype(jnp.float32)
        right = coded[:, rank:] * kept[:, None]
        sketch = jnp.dot(left.T, right, precision=lax.Precision.HIGHEST, preferred_element_type=jnp.float32)
        return sketch.reshape(rank * rank).astype(jnp.bfloat16)
    train = lax.map(one_example, (acts, grads, lengths))
    train_wide = lax.optimization_barrier(train).astype(jnp.float32)
    valid_wide = val_sketches.astype(jnp.float32)
    train_sq = lax.optimization_barrier(jnp.sum(train_wide * train_wide, axis=1))
    val_sq = lax.optimization_barrier(jnp.sum(valid_wide * valid_wide, axis=1))
    dots = jnp.dot(train_wide, valid_wide.T, precision=lax.Precision.HIGHEST, preferred_element_type=jnp.float32)
    factor = jnp.sqrt(jnp.float32(rank * rank))
    return dots * lax.rsqrt(train_sq + 1e-06)[:, None] * lax.rsqrt(val_sq + 1e-06)[None, :] * factor
```

```python
import functools

import jax
import jax.numpy as jnp
from jax import lax
from jax.experimental import pallas as pl
from jax.experimental.pallas import tpu as pltpu
from jax.sharding import PartitionSpec as P

MESH = pl.DeviceIdType.MESH
LANES = 128
TILE = 16


def columns(start, size):
    return pl.ds(start, size)


def kernel(sizes, act_hbm, grad_hbm, win_hbm, wout_hbm, len_hbm, val_hbm, out_ref,
           act, grad, win, wout, lens, val, half, half_in, wide, packed, landed, flat, query,
           squares, vsq, vsq_in, part, part_in,
           load_sem, val_sem, pair_send, pair_recv, sk_send, sk_recv, vsq_send, vsq_recv,
           part_send, part_recv):
    R, C, T = sizes
    r, c, t = lax.axis_index("row"), lax.axis_index("col"), lax.axis_index("tensor")
    me = r * C + c
    examples = lens.shape[0]
    slots = act.shape[0] // examples
    rank = win.shape[0]
    ff = act.shape[1]
    nv, own = val.shape
    group = C * examples
    groups = own // LANES
    chunks = load_sem.shape[0] - 4
    step = ff // chunks
    vchunks = val_sem.shape[0]
    vstep = nv // vchunks

    def loops(n, body):
        if n <= 8:
            for d in range(1, n):
                body(d)
        else:
            pl.loop(1, n)(body)

    barrier = pltpu.get_barrier_semaphore()

    def greet(d):
        other = lax.rem(me + d, R * C)
        pl.semaphore_signal(barrier, inc=1, device_id={"row": other // C, "col": lax.rem(other, C)},
                            device_id_type=MESH)

    loops(R * C, greet)
    for d in range(1, T):
        pl.semaphore_signal(barrier, inc=1, device_id={"tensor": lax.rem(t + d, T)}, device_id_type=MESH)

    loads = []
    for k in range(chunks):
        cut = columns(k * step, step)
        loads.append([
            pltpu.make_async_copy(act_hbm.at[:, cut], act.at[:, cut], load_sem.at[k, 0]),
            pltpu.make_async_copy(win_hbm.at[:, cut], win.at[:, cut], load_sem.at[k, 1]),
        ])
    tail = [
        pltpu.make_async_copy(grad_hbm, grad, load_sem.at[chunks, 0]),
        pltpu.make_async_copy(wout_hbm, wout.at[0:rank], load_sem.at[chunks + 1, 0]),
        pltpu.make_async_copy(wout_hbm, wout.at[rank:2 * rank], load_sem.at[chunks + 2, 0]),
        pltpu.make_async_copy(len_hbm, lens, load_sem.at[chunks + 3, 0]),
    ]
    vloads = [
        pltpu.make_async_copy(val_hbm.at[pl.ds(k * vstep, vstep)], val.at[pl.ds(k * vstep, vstep)],
                              val_sem.at[k])
        for k in range(vchunks)
    ]
    for copy in tail:
        copy.start()
    for pair in loads:
        for copy in pair:
            copy.start()
    for copy in vloads:
        copy.start()

    contract = (((1,), (1,)), ((), ()))
    for copy in tail:
        copy.wait()
    half[rank:, :] = lax.dot_general(grad[...], wout[...], contract, preferred_element_type=jnp.float32)
    total = None
    for k in range(chunks):
        for copy in loads[k]:
            copy.wait()
        cut = slice(k * step, (k + 1) * step)
        term = lax.dot_general(win[:, cut], act[:, cut], contract, preferred_element_type=jnp.float32)
        total = term if total is None else total + term
    half[0:rank, :] = total

    pl.semaphore_wait(barrier, R * C - 1 + T - 1)

    pairs = []
    for d in range(1, T):
        other = lax.rem(t + d, T)
        copy = pltpu.make_async_remote_copy(
            half, half_in.at[t], pair_send.at[d], pair_recv.at[t],
            device_id={"tensor": other}, device_id_type=MESH)
        copy.start()
        pairs.append(copy)

    def val_squares(k):
        vloads[k].wait()
        rows = 64
        for b in range(vstep // rows):
            base = k * vstep + b * rows
            acc = None
            for g in range(groups):
                x = val[base:base + rows, g * LANES:(g + 1) * LANES].astype(jnp.float32)
                acc = x * x if acc is None else acc + x * x
            squares[base:base + rows, :] = acc

    for k in range(vchunks // 2):
        val_squares(k)

    joined = half[...]
    for d in range(1, T):
        other = lax.rem(t + d, T)
        pltpu.make_async_remote_copy(
            half, half_in.at[other], pair_send.at[d], pair_recv.at[other],
            device_id={"tensor": other}, device_id_type=MESH).wait_recv()
        joined = joined + half_in[other]
    left_t = joined[0:rank].astype(jnp.bfloat16)
    right = joined[rank:].astype(jnp.bfloat16).astype(jnp.float32)
    slot = lax.broadcasted_iota(jnp.int32, right.shape, 0)
    blocks = []
    for e in range(examples):
        kept = (slot >= e * slots) & (slot < e * slots + lens[e])
        blocks.append(jnp.where(kept, right, 0.0).astype(jnp.bfloat16))
    wide_right = jnp.concatenate(blocks, axis=1)
    outer = jnp.dot(left_t, wide_right, preferred_element_type=jnp.float32)
    lane = lax.broadcasted_iota(jnp.int32, (rank // 2, LANES), 1)
    for e in range(examples):
        wide[e] = outer[:, e * LANES:(e + 1) * LANES]
    for e in range(examples):
        even = wide[e, pl.ds(0, rank // 2, stride=2), :]
        odd = wide[e, pl.ds(1, rank // 2, stride=2), :]
        sketch = jnp.where(lane < rank, even, odd).astype(jnp.bfloat16)
        for b in range(rank // 2 // TILE):
            packed[b, e] = sketch[b * TILE:(b + 1) * TILE]

    def tile_of(row):
        return (row * groups) // TILE

    def sketch_copy(d):
        other = lax.rem(me + d, R * C)
        return pltpu.make_async_remote_copy(
            packed.at[tile_of(other // C)], landed.at[me], sk_send.at[d], sk_recv.at[me],
            device_id={"row": other // C, "col": lax.rem(other, C)}, device_id_type=MESH)

    def sketch_arrival(d):
        other = lax.rem(me + d, R * C)
        return pltpu.make_async_remote_copy(
            packed.at[0], landed.at[other], sk_send.at[d], sk_recv.at[other],
            device_id={"row": other // C, "col": lax.rem(other, C)}, device_id_type=MESH)

    loops(R * C, lambda d: sketch_copy(d).start())

    for k in range(vchunks // 2, vchunks):
        val_squares(k)
    ones = jnp.ones((8, LANES), jnp.bfloat16)
    high = squares[...].astype(jnp.bfloat16)
    low = (squares[...] - high.astype(jnp.float32)).astype(jnp.bfloat16)
    sums = (lax.dot_general(ones, high, contract, preferred_element_type=jnp.float32)
            + lax.dot_general(ones, low, contract, preferred_element_type=jnp.float32))
    vsq[...] = sums[0:1]

    def vsq_copy(d, mine):
        other = lax.rem(r + d, R)
        at = r if mine else other
        return pltpu.make_async_remote_copy(
            vsq, vsq_in.at[at], vsq_send.at[d], vsq_recv.at[at],
            device_id={"row": other}, device_id_type=MESH)

    loops(R, lambda d: vsq_copy(d, True).start())

    flat[me] = packed[tile_of(r)].astype(jnp.float32)

    def take(d):
        other = lax.rem(me + d, R * C)
        sketch_arrival(d).wait_recv()
        flat[other] = landed[other].astype(jnp.float32)

    loops(R * C, take)

    offset = lax.rem(r * groups, TILE)
    rows = flat.reshape(R * C * examples * TILE, LANES)
    train_sq = jnp.zeros((R * C * examples, LANES), jnp.float32)
    for g in range(groups):
        piece = rows[pl.ds(offset + g, R * C * examples, stride=TILE), :]
        train_sq = train_sq + piece * piece
        query[:, g * LANES:(g + 1) * LANES] = piece.astype(jnp.bfloat16)
    part[:, :, 0:LANES] = train_sq.reshape(R, group, LANES)

    def part_copy(d, k, mine):
        other = lax.rem(r + d, R)
        at = r if mine else other
        cut = columns(0, LANES + vstep) if k == 0 else columns(LANES + k * vstep, vstep)
        return pltpu.make_async_remote_copy(
            part.at[other, :, cut], part_in.at[at, :, cut], part_send.at[d, k], part_recv.at[at, k],
            device_id={"row": other}, device_id_type=MESH)

    for k in range(vchunks):
        dots = lax.dot_general(query[...], val[k * vstep:(k + 1) * vstep, :], contract,
                               preferred_element_type=jnp.float32)
        part[:, :, LANES + k * vstep:LANES + (k + 1) * vstep] = dots.reshape(R, group, vstep)
        loops(R, lambda d: part_copy(d, k, True).start())

    factor = float(rank)

    def own_sum(cut, k):
        if R <= 8:
            total = part[r, :, cut]
            for d in range(1, R):
                total = total + part_in[lax.rem(r + d, R), :, cut]
            return total
        return lax.fori_loop(1, R, lambda d, a: a + part_in[lax.rem(r + d, R), :, cut], part[r, :, cut])

    loops(R, lambda d: vsq_copy(d, False).wait_recv())
    if R <= 8:
        val_sq = vsq[...]
        for d in range(1, R):
            val_sq = val_sq + vsq_in[lax.rem(r + d, R)]
    else:
        val_sq = lax.fori_loop(1, R, lambda d, a: a + vsq_in[lax.rem(r + d, R)], vsq[...])
    val_scale = lax.rsqrt(val_sq + 1e-06)
    train_scale = None
    for k in range(vchunks):
        loops(R, lambda d: part_copy(d, k, False).wait_recv())
        if k == 0:
            train = jnp.sum(own_sum(slice(0, LANES), 0), axis=1, keepdims=True)
            train_scale = lax.rsqrt(train + 1e-06) * factor
        dots = own_sum(slice(LANES + k * vstep, LANES + (k + 1) * vstep), k)
        out_ref[:, k * vstep:(k + 1) * vstep] = (
            dots * train_scale * val_scale[:, k * vstep:(k + 1) * vstep])

    for copy in pairs:
        copy.wait_send()
    loops(R * C, lambda d: sketch_copy(d).wait_send())
    loops(R, lambda d: vsq_copy(d, True).wait_send())
    for k in range(vchunks):
        loops(R, lambda d: part_copy(d, k, True).wait_send())


def on_device(sizes, activations, out_grads, proj_in, proj_out, lengths, val_sketches):
    R, C, T = sizes
    tokens, ff = activations.shape
    width = out_grads.shape[1]
    rank = proj_in.shape[1]
    examples = lengths.shape[0]
    nv, own = val_sketches.shape
    group = C * examples
    chunks, vchunks = 4, 4
    bf16, f32 = jnp.bfloat16, jnp.float32
    tiles = rank // 2 // TILE
    scratch = [
        pltpu.VMEM((tokens, ff), bf16),
        pltpu.VMEM((tokens, width), bf16),
        pltpu.VMEM((rank, ff), bf16),
        pltpu.VMEM((2 * rank, width), bf16),
        pltpu.SMEM((examples,), jnp.int32),
        pltpu.VMEM((nv, own), bf16),
        pltpu.VMEM((rank + tokens, LANES), f32),
        pltpu.VMEM((T, rank + tokens, LANES), f32),
        pltpu.VMEM((examples, rank, LANES), f32),
        pltpu.VMEM((tiles, examples, TILE, LANES), bf16),
        pltpu.VMEM((R * C, examples, TILE, LANES), bf16),
        pltpu.VMEM((R * C, examples, TILE, LANES), f32),
        pltpu.VMEM((R * C * examples, own), bf16),
        pltpu.VMEM((nv, LANES), f32),
        pltpu.VMEM((1, nv), f32),
        pltpu.VMEM((R, 1, nv), f32),
        pltpu.VMEM((R, group, LANES + nv), f32),
        pltpu.VMEM((R, group, LANES + nv), f32),
        pltpu.SemaphoreType.DMA((chunks + 4, 2)),
        pltpu.SemaphoreType.DMA((vchunks,)),
        pltpu.SemaphoreType.DMA((T,)),
        pltpu.SemaphoreType.DMA((T,)),
        pltpu.SemaphoreType.DMA((R * C,)),
        pltpu.SemaphoreType.DMA((R * C,)),
        pltpu.SemaphoreType.DMA((R,)),
        pltpu.SemaphoreType.DMA((R,)),
        pltpu.SemaphoreType.DMA((R, vchunks)),
        pltpu.SemaphoreType.DMA((R, vchunks)),
    ]
    return pl.pallas_call(
        functools.partial(kernel, sizes),
        out_shape=jax.ShapeDtypeStruct((group, nv), f32),
        in_specs=[pl.BlockSpec(memory_space=pl.ANY)] * 6,
        out_specs=pl.BlockSpec(memory_space=pltpu.VMEM),
        scratch_shapes=scratch,
        compiler_params=pltpu.CompilerParams(
            collective_id=0, has_side_effects=True, vmem_limit_bytes=40 * 1024 * 1024
        ),
    )(activations, out_grads, proj_in.T, proj_out.T, lengths, val_sketches)


def solution(mesh):
    sizes = (mesh.shape["row"], mesh.shape["col"], mesh.shape["tensor"])
    placed = (
        P(("groups", "row", "col"), "tensor"),
        P(("groups", "row", "col"), "tensor"),
        P("tensor", None),
        P("tensor", None),
        P(("groups", "row", "col")),
        P(("groups", "col", "tensor"), "row"),
    )
    return jax.shard_map(
        functools.partial(on_device, sizes),
        mesh=mesh,
        in_specs=placed,
        out_specs=P(("groups", "row"), ("col", "tensor")),
        check_vma=False,
    )
```

```python
import functools

import jax
import jax.numpy as jnp
from jax import lax
from jax.experimental import pallas as pl
from jax.experimental.pallas import tpu as pltpu
from jax.sharding import PartitionSpec as P

MESH = pl.DeviceIdType.MESH
LANES = 128
TILE = 16


def columns(start, size):
    return pl.ds(start, size)


def kernel(sizes, act_hbm, grad_hbm, win_hbm, wout_hbm, len_hbm, val_hbm, out_ref,
           act, grad, win, wout, lens, val, half, half_in, wide, packed, landed, flat, query,
           squares, vsq, vsq_in, part, part_in,
           load_sem, val_sem, pair_send, pair_recv, sk_send, sk_recv, vsq_send, vsq_recv,
           part_send, part_recv):
    R, C, T = sizes
    r, c, t = lax.axis_index("row"), lax.axis_index("col"), lax.axis_index("tensor")
    me = r * C + c
    examples = lens.shape[0]
    slots = act.shape[0] // examples
    rank = win.shape[0]
    ff = act.shape[1]
    nv, own = val.shape
    group = C * examples
    groups = own // LANES
    chunks = load_sem.shape[0] - 4
    step = ff // chunks
    vchunks = val_sem.shape[0]
    vstep = nv // vchunks

    def loops(n, body):
        if n <= 8:
            for d in range(1, n):
                body(d)
        else:
            pl.loop(1, n)(body)

    barrier = pltpu.get_barrier_semaphore()

    def greet(d):
        other = lax.rem(me + d, R * C)
        pl.semaphore_signal(barrier, inc=1, device_id={"row": other // C, "col": lax.rem(other, C)},
                            device_id_type=MESH)

    loops(R * C, greet)
    for d in range(1, T):
        pl.semaphore_signal(barrier, inc=1, device_id={"tensor": lax.rem(t + d, T)}, device_id_type=MESH)

    loads = []
    for k in range(chunks):
        cut = columns(k * step, step)
        loads.append([
            pltpu.make_async_copy(act_hbm.at[:, cut], act.at[:, cut], load_sem.at[k, 0]),
            pltpu.make_async_copy(win_hbm.at[:, cut], win.at[:, cut], load_sem.at[k, 1]),
        ])
    tail = [
        pltpu.make_async_copy(grad_hbm, grad, load_sem.at[chunks, 0]),
        pltpu.make_async_copy(wout_hbm, wout.at[0:rank], load_sem.at[chunks + 1, 0]),
        pltpu.make_async_copy(wout_hbm, wout.at[rank:2 * rank], load_sem.at[chunks + 2, 0]),
        pltpu.make_async_copy(len_hbm, lens, load_sem.at[chunks + 3, 0]),
    ]
    vloads = [
        pltpu.make_async_copy(val_hbm.at[pl.ds(k * vstep, vstep)], val.at[pl.ds(k * vstep, vstep)],
                              val_sem.at[k])
        for k in range(vchunks)
    ]
    for copy in tail:
        copy.start()
    for pair in loads:
        for copy in pair:
            copy.start()
    for copy in vloads:
        copy.start()

    contract = (((1,), (1,)), ((), ()))
    for copy in tail:
        copy.wait()
    half[rank:, :] = lax.dot_general(grad[...], wout[...], contract, preferred_element_type=jnp.float32)
    total = None
    for k in range(chunks):
        for copy in loads[k]:
            copy.wait()
        cut = slice(k * step, (k + 1) * step)
        term = lax.dot_general(win[:, cut], act[:, cut], contract, preferred_element_type=jnp.float32)
        total = term if total is None else total + term
    half[0:rank, :] = total

    pl.semaphore_wait(barrier, R * C - 1 + T - 1)

    pairs = []
    for d in range(1, T):
        other = lax.rem(t + d, T)
        copy = pltpu.make_async_remote_copy(
            half, half_in.at[t], pair_send.at[d], pair_recv.at[t],
            device_id={"tensor": other}, device_id_type=MESH)
        copy.start()
        pairs.append(copy)

    def val_squares(k):
        vloads[k].wait()
        rows = 64
        for b in range(vstep // rows):
            base = k * vstep + b * rows
            acc = None
            for g in range(groups):
                x = val[base:base + rows, g * LANES:(g + 1) * LANES].astype(jnp.float32)
                acc = x * x if acc is None else acc + x * x
            squares[base:base + rows, :] = acc

    for k in range(vchunks // 2):
        val_squares(k)

    joined = half[...]
    for d in range(1, T):
        other = lax.rem(t + d, T)
        pltpu.make_async_remote_copy(
            half, half_in.at[other], pair_send.at[d], pair_recv.at[other],
            device_id={"tensor": other}, device_id_type=MESH).wait_recv()
        joined = joined + half_in[other]
    left_t = joined[0:rank].astype(jnp.bfloat16)
    right = joined[rank:].astype(jnp.bfloat16).astype(jnp.float32)
    slot = lax.broadcasted_iota(jnp.int32, right.shape, 0)
    blocks = []
    for e in range(examples):
        kept = (slot >= e * slots) & (slot < e * slots + lens[e])
        blocks.append(jnp.where(kept, right, 0.0).astype(jnp.bfloat16))
    wide_right = jnp.concatenate(blocks, axis=1)
    outer = jnp.dot(left_t, wide_right, preferred_element_type=jnp.float32)
    lane = lax.broadcasted_iota(jnp.int32, (rank // 2, LANES), 1)
    for e in range(examples):
        wide[e] = outer[:, e * LANES:(e + 1) * LANES]
    for e in range(examples):
        even = wide[e, pl.ds(0, rank // 2, stride=2), :]
        odd = wide[e, pl.ds(1, rank // 2, stride=2), :]
        sketch = jnp.where(lane < rank, even, odd).astype(jnp.bfloat16)
        for b in range(rank // 2 // TILE):
            packed[b, e] = sketch[b * TILE:(b + 1) * TILE]

    def tile_of(row):
        return (row * groups) // TILE

    def sketch_copy(d):
        other = lax.rem(me + d, R * C)
        return pltpu.make_async_remote_copy(
            packed.at[tile_of(other // C)], landed.at[me], sk_send.at[d], sk_recv.at[me],
            device_id={"row": other // C, "col": lax.rem(other, C)}, device_id_type=MESH)

    def sketch_arrival(d):
        other = lax.rem(me + d, R * C)
        return pltpu.make_async_remote_copy(
            packed.at[0], landed.at[other], sk_send.at[d], sk_recv.at[other],
            device_id={"row": other // C, "col": lax.rem(other, C)}, device_id_type=MESH)

    loops(R * C, lambda d: sketch_copy(d).start())

    for k in range(vchunks // 2, vchunks):
        val_squares(k)
    ones = jnp.ones((8, LANES), jnp.bfloat16)
    high = squares[...].astype(jnp.bfloat16)
    low = (squares[...] - high.astype(jnp.float32)).astype(jnp.bfloat16)
    sums = (lax.dot_general(ones, high, contract, preferred_element_type=jnp.float32)
            + lax.dot_general(ones, low, contract, preferred_element_type=jnp.float32))
    vsq[...] = sums[0:1]

    def vsq_copy(d, mine):
        other = lax.rem(r + d, R)
        at = r if mine else other
        return pltpu.make_async_remote_copy(
            vsq, vsq_in.at[at], vsq_send.at[d], vsq_recv.at[at],
            device_id={"row": other}, device_id_type=MESH)

    loops(R, lambda d: vsq_copy(d, True).start())

    flat[me] = packed[tile_of(r)].astype(jnp.float32)

    def take(d):
        other = lax.rem(me + d, R * C)
        sketch_arrival(d).wait_recv()
        flat[other] = landed[other].astype(jnp.float32)

    loops(R * C, take)

    offset = lax.rem(r * groups, TILE)
    rows = flat.reshape(R * C * examples * TILE, LANES)
    train_sq = jnp.zeros((R * C * examples, LANES), jnp.float32)
    for g in range(groups):
        piece = rows[pl.ds(offset + g, R * C * examples, stride=TILE), :]
        train_sq = train_sq + piece * piece
        query[:, g * LANES:(g + 1) * LANES] = piece.astype(jnp.bfloat16)
    part[:, :, 0:LANES] = train_sq.reshape(R, group, LANES)

    def part_copy(d, k, mine):
        other = lax.rem(r + d, R)
        at = r if mine else other
        cut = columns(0, LANES + vstep) if k == 0 else columns(LANES + k * vstep, vstep)
        return pltpu.make_async_remote_copy(
            part.at[other, :, cut], part_in.at[at, :, cut], part_send.at[d, k], part_recv.at[at, k],
            device_id={"row": other}, device_id_type=MESH)

    for k in range(vchunks):
        dots = lax.dot_general(query[...], val[k * vstep:(k + 1) * vstep, :], contract,
                               preferred_element_type=jnp.float32)
        part[:, :, LANES + k * vstep:LANES + (k + 1) * vstep] = dots.reshape(R, group, vstep)
        loops(R, lambda d: part_copy(d, k, True).start())

    factor = float(rank)

    def own_sum(cut, k):
        if R <= 8:
            total = part[r, :, cut]
            for d in range(1, R):
                total = total + part_in[lax.rem(r + d, R), :, cut]
            return total
        return lax.fori_loop(1, R, lambda d, a: a + part_in[lax.rem(r + d, R), :, cut], part[r, :, cut])

    loops(R, lambda d: vsq_copy(d, False).wait_recv())
    if R <= 8:
        val_sq = vsq[...]
        for d in range(1, R):
            val_sq = val_sq + vsq_in[lax.rem(r + d, R)]
    else:
        val_sq = lax.fori_loop(1, R, lambda d, a: a + vsq_in[lax.rem(r + d, R)], vsq[...])
    val_scale = lax.rsqrt(val_sq + 1e-06)
    train_scale = None
    for k in range(vchunks):
        loops(R, lambda d: part_copy(d, k, False).wait_recv())
        if k == 0:
            train = jnp.sum(own_sum(slice(0, LANES), 0), axis=1, keepdims=True)
            train_scale = lax.rsqrt(train + 1e-06) * factor
        dots = own_sum(slice(LANES + k * vstep, LANES + (k + 1) * vstep), k)
        out_ref[:, k * vstep:(k + 1) * vstep] = (
            dots * train_scale * val_scale[:, k * vstep:(k + 1) * vstep])

    for copy in pairs:
        copy.wait_send()
    loops(R * C, lambda d: sketch_copy(d).wait_send())
    loops(R, lambda d: vsq_copy(d, True).wait_send())
    for k in range(vchunks):
        loops(R, lambda d: part_copy(d, k, True).wait_send())


def on_device(sizes, activations, out_grads, proj_in, proj_out, lengths, val_sketches):
    R, C, T = sizes
    tokens, ff = activations.shape
    width = out_grads.shape[1]
    rank = proj_in.shape[1]
    examples = lengths.shape[0]
    nv, own = val_sketches.shape
    group = C * examples
    chunks, vchunks = 4, 4
    bf16, f32 = jnp.bfloat16, jnp.float32
    tiles = rank // 2 // TILE
    scratch = [
        pltpu.VMEM((tokens, ff), bf16),
        pltpu.VMEM((tokens, width), bf16),
        pltpu.VMEM((rank, ff), bf16),
        pltpu.VMEM((2 * rank, width), bf16),
        pltpu.SMEM((examples,), jnp.int32),
        pltpu.VMEM((nv, own), bf16),
        pltpu.VMEM((rank + tokens, LANES), f32),
        pltpu.VMEM((T, rank + tokens, LANES), f32),
        pltpu.VMEM((examples, rank, LANES), f32),
        pltpu.VMEM((tiles, examples, TILE, LANES), bf16),
        pltpu.VMEM((R * C, examples, TILE, LANES), bf16),
        pltpu.VMEM((R * C, examples, TILE, LANES), f32),
        pltpu.VMEM((R * C * examples, own), bf16),
        pltpu.VMEM((nv, LANES), f32),
        pltpu.VMEM((1, nv), f32),
        pltpu.VMEM((R, 1, nv), f32),
        pltpu.VMEM((R, group, LANES + nv), f32),
        pltpu.VMEM((R, group, LANES + nv), f32),
        pltpu.SemaphoreType.DMA((chunks + 4, 2)),
        pltpu.SemaphoreType.DMA((vchunks,)),
        pltpu.SemaphoreType.DMA((T,)),
        pltpu.SemaphoreType.DMA((T,)),
        pltpu.SemaphoreType.DMA((R * C,)),
        pltpu.SemaphoreType.DMA((R * C,)),
        pltpu.SemaphoreType.DMA((R,)),
        pltpu.SemaphoreType.DMA((R,)),
        pltpu.SemaphoreType.DMA((R, vchunks)),
        pltpu.SemaphoreType.DMA((R, vchunks)),
    ]
    return pl.pallas_call(
        functools.partial(kernel, sizes),
        out_shape=jax.ShapeDtypeStruct((group, nv), f32),
        in_specs=[pl.BlockSpec(memory_space=pltpu.HBM)] * 6,
        out_specs=pl.BlockSpec(memory_space=pltpu.VMEM),
        scratch_shapes=scratch,
        compiler_params=pltpu.CompilerParams(
            collective_id=0, has_side_effects=True, vmem_limit_bytes=56 * 1024 * 1024
        ),
    )(activations, out_grads, proj_in.T, proj_out.T, lengths, val_sketches)


def solution(mesh):
    sizes = (mesh.shape["row"], mesh.shape["col"], mesh.shape["tensor"])
    placed = (
        P(("groups", "row", "col"), "tensor"),
        P(("groups", "row", "col"), "tensor"),
        P("tensor", None),
        P("tensor", None),
        P(("groups", "row", "col")),
        P(("groups", "col", "tensor"), "row"),
    )
    return jax.shard_map(
        functools.partial(on_device, sizes),
        mesh=mesh,
        in_specs=placed,
        out_specs=P(("groups", "row"), ("col", "tensor")),
        check_vma=False,
    )
```

```python
import functools

import jax
import jax.numpy as jnp
from jax import lax
from jax.experimental import pallas as pl
from jax.experimental.pallas import tpu as pltpu
from jax.sharding import PartitionSpec as P

MESH = pl.DeviceIdType.MESH
LANES = 128
TILE = 16


def columns(start, size):
    return pl.ds(start, size)


def kernel(sizes, act_hbm, grad_hbm, win_hbm, wout_hbm, len_hbm, val_hbm, out_ref,
           act, grad, win, wout, lens, val, half, half_in, wide, packed, landed, flat, query,
           squares, vsq, vsq_in, part, part_in,
           load_sem, val_sem, pair_send, pair_recv, sk_send, sk_recv, vsq_send, vsq_recv,
           part_send, part_recv):
    R, C, T = sizes
    r, c, t = lax.axis_index("row"), lax.axis_index("col"), lax.axis_index("tensor")
    me = r * C + c
    examples = lens.shape[0]
    slots = act.shape[0] // examples
    rank = win.shape[0]
    ff = act.shape[1]
    nv, own = val.shape
    group = C * examples
    groups = own // LANES
    chunks = load_sem.shape[0] - 4
    step = ff // chunks
    vchunks = val_sem.shape[0]
    vstep = nv // vchunks

    def loops(n, body):
        if n <= 8:
            for d in range(1, n):
                body(d)
        else:
            pl.loop(1, n)(body)

    barrier = pltpu.get_barrier_semaphore()

    def greet(d):
        other = lax.rem(me + d, R * C)
        pl.semaphore_signal(barrier, inc=1, device_id={"row": other // C, "col": lax.rem(other, C)},
                            device_id_type=MESH)

    loops(R * C, greet)
    for d in range(1, T):
        pl.semaphore_signal(barrier, inc=1, device_id={"tensor": lax.rem(t + d, T)}, device_id_type=MESH)

    loads = []
    for k in range(chunks):
        cut = columns(k * step, step)
        loads.append([
            pltpu.make_async_copy(act_hbm.at[:, cut], act.at[:, cut], load_sem.at[k, 0]),
            pltpu.make_async_copy(win_hbm.at[:, cut], win.at[:, cut], load_sem.at[k, 1]),
        ])
    tail = [
        pltpu.make_async_copy(grad_hbm, grad, load_sem.at[chunks, 0]),
        pltpu.make_async_copy(wout_hbm, wout.at[0:rank], load_sem.at[chunks + 1, 0]),
        pltpu.make_async_copy(wout_hbm, wout.at[rank:2 * rank], load_sem.at[chunks + 2, 0]),
        pltpu.make_async_copy(len_hbm, lens, load_sem.at[chunks + 3, 0]),
    ]
    vloads = [
        pltpu.make_async_copy(val_hbm.at[pl.ds(k * vstep, vstep)], val.at[pl.ds(k * vstep, vstep)],
                              val_sem.at[k])
        for k in range(vchunks)
    ]
    for copy in tail:
        copy.start()
    for pair in loads:
        for copy in pair:
            copy.start()
    for copy in vloads:
        copy.start()

    contract = (((1,), (1,)), ((), ()))
    for copy in tail:
        copy.wait()
    half[rank:, :] = lax.dot_general(grad[...], wout[...], contract, preferred_element_type=jnp.float32)
    total = None
    for k in range(chunks):
        for copy in loads[k]:
            copy.wait()
        cut = slice(k * step, (k + 1) * step)
        term = lax.dot_general(win[:, cut], act[:, cut], contract, preferred_element_type=jnp.float32)
        total = term if total is None else total + term
    half[0:rank, :] = total

    pl.semaphore_wait(barrier, R * C - 1 + T - 1)

    pairs = []
    for d in range(1, T):
        other = lax.rem(t + d, T)
        copy = pltpu.make_async_remote_copy(
            half, half_in.at[t], pair_send.at[d], pair_recv.at[t],
            device_id={"tensor": other}, device_id_type=MESH)
        copy.start()
        pairs.append(copy)

    def val_squares(k):
        vloads[k].wait()
        rows = 64
        for b in range(vstep // rows):
            base = k * vstep + b * rows
            acc = None
            for g in range(groups):
                x = val[base:base + rows, g * LANES:(g + 1) * LANES].astype(jnp.float32)
                acc = x * x if acc is None else acc + x * x
            squares[base:base + rows, :] = acc

    for k in range(vchunks // 2):
        val_squares(k)

    joined = half[...]
    for d in range(1, T):
        other = lax.rem(t + d, T)
        pltpu.make_async_remote_copy(
            half, half_in.at[other], pair_send.at[d], pair_recv.at[other],
            device_id={"tensor": other}, device_id_type=MESH).wait_recv()
        joined = joined + half_in[other]
    left_t = joined[0:rank].astype(jnp.bfloat16)
    right = joined[rank:].astype(jnp.bfloat16).astype(jnp.float32)
    slot = lax.broadcasted_iota(jnp.int32, right.shape, 0)
    blocks = []
    for e in range(examples):
        kept = (slot >= e * slots) & (slot < e * slots + lens[e])
        blocks.append(jnp.where(kept, right, 0.0).astype(jnp.bfloat16))
    wide_right = jnp.concatenate(blocks, axis=1)
    outer = jnp.dot(left_t, wide_right, preferred_element_type=jnp.float32)
    lane = lax.broadcasted_iota(jnp.int32, (rank // 2, LANES), 1)
    for e in range(examples):
        wide[e] = outer[:, e * LANES:(e + 1) * LANES]
    for e in range(examples):
        even = wide[e, pl.ds(0, rank // 2, stride=2), :]
        odd = wide[e, pl.ds(1, rank // 2, stride=2), :]
        sketch = jnp.where(lane < rank, even, odd).astype(jnp.bfloat16)
        for b in range(rank // 2 // TILE):
            packed[b, e] = sketch[b * TILE:(b + 1) * TILE]

    def tile_of(row):
        return (row * groups) // TILE

    def sketch_copy(d):
        other = lax.rem(me + d, R * C)
        return pltpu.make_async_remote_copy(
            packed.at[tile_of(other // C)], landed.at[me], sk_send.at[d], sk_recv.at[me],
            device_id={"row": other // C, "col": lax.rem(other, C)}, device_id_type=MESH)

    def sketch_arrival(d):
        other = lax.rem(me + d, R * C)
        return pltpu.make_async_remote_copy(
            packed.at[0], landed.at[other], sk_send.at[d], sk_recv.at[other],
            device_id={"row": other // C, "col": lax.rem(other, C)}, device_id_type=MESH)

    loops(R * C, lambda d: sketch_copy(d).start())

    for k in range(vchunks // 2, vchunks):
        val_squares(k)
    ones = jnp.ones((8, LANES), jnp.bfloat16)
    high = squares[...].astype(jnp.bfloat16)
    low = (squares[...] - high.astype(jnp.float32)).astype(jnp.bfloat16)
    sums = (lax.dot_general(ones, high, contract, preferred_element_type=jnp.float32)
            + lax.dot_general(ones, low, contract, preferred_element_type=jnp.float32))
    vsq[...] = sums[0:1]

    def vsq_copy(d, mine):
        other = lax.rem(r + d, R)
        at = r if mine else other
        return pltpu.make_async_remote_copy(
            vsq, vsq_in.at[at], vsq_send.at[d], vsq_recv.at[at],
            device_id={"row": other}, device_id_type=MESH)

    loops(R, lambda d: vsq_copy(d, True).start())

    flat[me] = packed[tile_of(r)].astype(jnp.float32)

    def take(d):
        other = lax.rem(me + d, R * C)
        sketch_arrival(d).wait_recv()
        flat[other] = landed[other].astype(jnp.float32)

    loops(R * C, take)

    offset = lax.rem(r * groups, TILE)
    rows = flat.reshape(R * C * examples * TILE, LANES)
    train_sq = jnp.zeros((R * C * examples, LANES), jnp.float32)
    for g in range(groups):
        piece = rows[pl.ds(offset + g, R * C * examples, stride=TILE), :]
        train_sq = train_sq + piece * piece
        query[:, g * LANES:(g + 1) * LANES] = piece.astype(jnp.bfloat16)
    part[:, :, 0:LANES] = train_sq.reshape(R, group, LANES)

    def part_copy(d, k, mine):
        other = lax.rem(r + d, R)
        at = r if mine else other
        cut = columns(0, LANES + vstep) if k == 0 else columns(LANES + k * vstep, vstep)
        return pltpu.make_async_remote_copy(
            part.at[other, :, cut], part_in.at[at, :, cut], part_send.at[d, k], part_recv.at[at, k],
            device_id={"row": other}, device_id_type=MESH)

    for k in range(vchunks):
        dots = lax.dot_general(query[...], val[k * vstep:(k + 1) * vstep, :], contract,
                               preferred_element_type=jnp.float32)
        part[:, :, LANES + k * vstep:LANES + (k + 1) * vstep] = dots.reshape(R, group, vstep)
        loops(R, lambda d: part_copy(d, k, True).start())

    factor = float(rank)

    def own_sum(cut, k):
        if R <= 8:
            total = part[r, :, cut]
            for d in range(1, R):
                total = total + part_in[lax.rem(r + d, R), :, cut]
            return total
        return lax.fori_loop(1, R, lambda d, a: a + part_in[lax.rem(r + d, R), :, cut], part[r, :, cut])

    loops(R, lambda d: vsq_copy(d, False).wait_recv())
    if R <= 8:
        val_sq = vsq[...]
        for d in range(1, R):
            val_sq = val_sq + vsq_in[lax.rem(r + d, R)]
    else:
        val_sq = lax.fori_loop(1, R, lambda d, a: a + vsq_in[lax.rem(r + d, R)], vsq[...])
    val_scale = lax.rsqrt(val_sq + 1e-06)
    train_scale = None
    for k in range(vchunks):
        loops(R, lambda d: part_copy(d, k, False).wait_recv())
        if k == 0:
            train = jnp.sum(own_sum(slice(0, LANES), 0), axis=1, keepdims=True)
            train_scale = lax.rsqrt(train + 1e-06) * factor
        dots = own_sum(slice(LANES + k * vstep, LANES + (k + 1) * vstep), k)
        out_ref[:, k * vstep:(k + 1) * vstep] = (
            dots * train_scale * val_scale[:, k * vstep:(k + 1) * vstep])

    for copy in pairs:
        copy.wait_send()
    loops(R * C, lambda d: sketch_copy(d).wait_send())
    loops(R, lambda d: vsq_copy(d, True).wait_send())
    for k in range(vchunks):
        loops(R, lambda d: part_copy(d, k, True).wait_send())


def on_device(sizes, activations, out_grads, proj_in, proj_out, lengths, val_sketches):
    R, C, T = sizes
    tokens, ff = activations.shape
    width = out_grads.shape[1]
    rank = proj_in.shape[1]
    examples = lengths.shape[0]
    nv, own = val_sketches.shape
    group = C * examples
    chunks, vchunks = 4, 2
    bf16, f32 = jnp.bfloat16, jnp.float32
    tiles = rank // 2 // TILE
    scratch = [
        pltpu.VMEM((tokens, ff), bf16),
        pltpu.VMEM((tokens, width), bf16),
        pltpu.VMEM((rank, ff), bf16),
        pltpu.VMEM((2 * rank, width), bf16),
        pltpu.SMEM((examples,), jnp.int32),
        pltpu.VMEM((nv, own), bf16),
        pltpu.VMEM((rank + tokens, LANES), f32),
        pltpu.VMEM((T, rank + tokens, LANES), f32),
        pltpu.VMEM((examples, rank, LANES), f32),
        pltpu.VMEM((tiles, examples, TILE, LANES), bf16),
        pltpu.VMEM((R * C, examples, TILE, LANES), bf16),
        pltpu.VMEM((R * C, examples, TILE, LANES), f32),
        pltpu.VMEM((R * C * examples, own), bf16),
        pltpu.VMEM((nv, LANES), f32),
        pltpu.VMEM((1, nv), f32),
        pltpu.VMEM((R, 1, nv), f32),
        pltpu.VMEM((R, group, LANES + nv), f32),
        pltpu.VMEM((R, group, LANES + nv), f32),
        pltpu.SemaphoreType.DMA((chunks + 4, 2)),
        pltpu.SemaphoreType.DMA((vchunks,)),
        pltpu.SemaphoreType.DMA((T,)),
        pltpu.SemaphoreType.DMA((T,)),
        pltpu.SemaphoreType.DMA((R * C,)),
        pltpu.SemaphoreType.DMA((R * C,)),
        pltpu.SemaphoreType.DMA((R,)),
        pltpu.SemaphoreType.DMA((R,)),
        pltpu.SemaphoreType.DMA((R, vchunks)),
        pltpu.SemaphoreType.DMA((R, vchunks)),
    ]
    return pl.pallas_call(
        functools.partial(kernel, sizes),
        out_shape=jax.ShapeDtypeStruct((group, nv), f32),
        in_specs=[pl.BlockSpec(memory_space=pltpu.HBM)] * 6,
        out_specs=pl.BlockSpec(memory_space=pltpu.VMEM),
        scratch_shapes=scratch,
        compiler_params=pltpu.CompilerParams(
            collective_id=0, has_side_effects=True, vmem_limit_bytes=32 * 1024 * 1024
        ),
    )(*[pltpu.with_memory_space_constraint(x, pltpu.HBM) for x in
        (activations, out_grads, proj_in.T, proj_out.T, lengths, val_sketches)])


def solution(mesh):
    sizes = (mesh.shape["row"], mesh.shape["col"], mesh.shape["tensor"])
    placed = (
        P(("groups", "row", "col"), "tensor"),
        P(("groups", "row", "col"), "tensor"),
        P("tensor", None),
        P("tensor", None),
        P(("groups", "row", "col")),
        P(("groups", "col", "tensor"), "row"),
    )
    return jax.shard_map(
        functools.partial(on_device, sizes),
        mesh=mesh,
        in_specs=placed,
        out_specs=P(("groups", "row"), ("col", "tensor")),
        check_vma=False,
    )
```

```python
import functools

import jax
import jax.numpy as jnp
from jax import lax
from jax.experimental import pallas as pl
from jax.experimental.pallas import tpu as pltpu
from jax.sharding import PartitionSpec as P

MESH = pl.DeviceIdType.MESH
LANES = 128
TILE = 16


def columns(start, size):
    return pl.ds(start, size)


def kernel(sizes, act_hbm, grad_hbm, win_hbm, wout_hbm, len_hbm, val_hbm, out_ref,
           act, grad, win, wout, lens, val, half, half_in, wide, packed, landed, flat, query,
           squares, vsq, vsq_in, part, part_in,
           load_sem, val_sem, pair_send, pair_recv, sk_send, sk_recv, vsq_send, vsq_recv,
           part_send, part_recv):
    R, C, T = sizes
    r, c, t = lax.axis_index("row"), lax.axis_index("col"), lax.axis_index("tensor")
    me = r * C + c
    examples = lens.shape[0]
    slots = act.shape[0] // examples
    rank = win.shape[0]
    ff = act.shape[1]
    nv, own = val.shape
    group = C * examples
    groups = own // LANES
    chunks = load_sem.shape[0] - 4
    step = ff // chunks
    vchunks = val_sem.shape[0]
    vstep = nv // vchunks

    def loops(n, body):
        if n <= 8:
            for d in range(1, n):
                body(d)
        else:
            pl.loop(1, n)(body)

    barrier = pltpu.get_barrier_semaphore()

    def greet(d):
        other = lax.rem(me + d, R * C)
        pl.semaphore_signal(barrier, inc=1, device_id={"row": other // C, "col": lax.rem(other, C)},
                            device_id_type=MESH)

    loops(R * C, greet)
    for d in range(1, T):
        pl.semaphore_signal(barrier, inc=1, device_id={"tensor": lax.rem(t + d, T)}, device_id_type=MESH)

    loads = []
    for k in range(chunks):
        cut = columns(k * step, step)
        loads.append([
            pltpu.make_async_copy(act_hbm.at[:, cut], act.at[:, cut], load_sem.at[k, 0]),
            pltpu.make_async_copy(win_hbm.at[:, cut], win.at[:, cut], load_sem.at[k, 1]),
        ])
    tail = [
        pltpu.make_async_copy(grad_hbm, grad, load_sem.at[chunks, 0]),
        pltpu.make_async_copy(wout_hbm, wout.at[0:rank], load_sem.at[chunks + 1, 0]),
        pltpu.make_async_copy(wout_hbm, wout.at[rank:2 * rank], load_sem.at[chunks + 2, 0]),
        pltpu.make_async_copy(len_hbm, lens, load_sem.at[chunks + 3, 0]),
    ]
    vloads = [
        pltpu.make_async_copy(val_hbm.at[pl.ds(k * vstep, vstep)], val.at[pl.ds(k * vstep, vstep)],
                              val_sem.at[k])
        for k in range(vchunks)
    ]
    for copy in tail:
        copy.start()
    for pair in loads:
        for copy in pair:
            copy.start()

    contract = (((1,), (1,)), ((), ()))
    for copy in tail:
        copy.wait()
    half[rank:, :] = lax.dot_general(grad[...], wout[...], contract, preferred_element_type=jnp.float32)
    total = None
    for k in range(chunks):
        for copy in loads[k]:
            copy.wait()
        if k == chunks - 1:
            for copy in vloads:
                copy.start()
        cut = slice(k * step, (k + 1) * step)
        term = lax.dot_general(win[:, cut], act[:, cut], contract, preferred_element_type=jnp.float32)
        total = term if total is None else total + term
    half[0:rank, :] = total

    pl.semaphore_wait(barrier, R * C - 1 + T - 1)

    pairs = []
    for d in range(1, T):
        other = lax.rem(t + d, T)
        copy = pltpu.make_async_remote_copy(
            half, half_in.at[t], pair_send.at[d], pair_recv.at[t],
            device_id={"tensor": other}, device_id_type=MESH)
        copy.start()
        pairs.append(copy)

    def val_squares(k):
        vloads[k].wait()
        rows = 64
        for b in range(vstep // rows):
            base = k * vstep + b * rows
            acc = None
            for g in range(groups):
                x = val[base:base + rows, g * LANES:(g + 1) * LANES].astype(jnp.float32)
                acc = x * x if acc is None else acc + x * x
            squares[base:base + rows, :] = acc


    joined = half[...]
    for d in range(1, T):
        other = lax.rem(t + d, T)
        pltpu.make_async_remote_copy(
            half, half_in.at[other], pair_send.at[d], pair_recv.at[other],
            device_id={"tensor": other}, device_id_type=MESH).wait_recv()
        joined = joined + half_in[other]
    left_t = joined[0:rank].astype(jnp.bfloat16)
    right = joined[rank:].astype(jnp.bfloat16).astype(jnp.float32)
    slot = lax.broadcasted_iota(jnp.int32, right.shape, 0)
    blocks = []
    for e in range(examples):
        kept = (slot >= e * slots) & (slot < e * slots + lens[e])
        blocks.append(jnp.where(kept, right, 0.0).astype(jnp.bfloat16))
    wide_right = jnp.concatenate(blocks, axis=1)
    outer = jnp.dot(left_t, wide_right, preferred_element_type=jnp.float32)
    lane = lax.broadcasted_iota(jnp.int32, (rank // 2, LANES), 1)
    for e in range(examples):
        wide[e] = outer[:, e * LANES:(e + 1) * LANES]
    for e in range(examples):
        even = wide[e, pl.ds(0, rank // 2, stride=2), :]
        odd = wide[e, pl.ds(1, rank // 2, stride=2), :]
        sketch = jnp.where(lane < rank, even, odd).astype(jnp.bfloat16)
        for b in range(rank // 2 // TILE):
            packed[b, e] = sketch[b * TILE:(b + 1) * TILE]

    def tile_of(row):
        return (row * groups) // TILE

    def sketch_copy(d):
        other = lax.rem(me + d, R * C)
        return pltpu.make_async_remote_copy(
            packed.at[tile_of(other // C)], landed.at[me], sk_send.at[d], sk_recv.at[me],
            device_id={"row": other // C, "col": lax.rem(other, C)}, device_id_type=MESH)

    def sketch_arrival(d):
        other = lax.rem(me + d, R * C)
        return pltpu.make_async_remote_copy(
            packed.at[0], landed.at[other], sk_send.at[d], sk_recv.at[other],
            device_id={"row": other // C, "col": lax.rem(other, C)}, device_id_type=MESH)

    loops(R * C, lambda d: sketch_copy(d).start())

    for k in range(vchunks):
        val_squares(k)
    ones = jnp.ones((8, LANES), jnp.bfloat16)
    high = squares[...].astype(jnp.bfloat16)
    low = (squares[...] - high.astype(jnp.float32)).astype(jnp.bfloat16)
    sums = (lax.dot_general(ones, high, contract, preferred_element_type=jnp.float32)
            + lax.dot_general(ones, low, contract, preferred_element_type=jnp.float32))
    vsq[...] = sums[0:1]

    def vsq_copy(d, mine):
        other = lax.rem(r + d, R)
        at = r if mine else other
        return pltpu.make_async_remote_copy(
            vsq, vsq_in.at[at], vsq_send.at[d], vsq_recv.at[at],
            device_id={"row": other}, device_id_type=MESH)

    loops(R, lambda d: vsq_copy(d, True).start())

    flat[me] = packed[tile_of(r)].astype(jnp.float32)

    def take(d):
        other = lax.rem(me + d, R * C)
        sketch_arrival(d).wait_recv()
        flat[other] = landed[other].astype(jnp.float32)

    loops(R * C, take)

    offset = lax.rem(r * groups, TILE)
    rows = flat.reshape(R * C * examples * TILE, LANES)
    train_sq = jnp.zeros((R * C * examples, LANES), jnp.float32)
    for g in range(groups):
        piece = rows[pl.ds(offset + g, R * C * examples, stride=TILE), :]
        train_sq = train_sq + piece * piece
        query[:, g * LANES:(g + 1) * LANES] = piece.astype(jnp.bfloat16)
    part[:, :, 0:LANES] = train_sq.reshape(R, group, LANES)

    def part_copy(d, k, mine):
        other = lax.rem(r + d, R)
        at = r if mine else other
        cut = columns(0, LANES + vstep) if k == 0 else columns(LANES + k * vstep, vstep)
        return pltpu.make_async_remote_copy(
            part.at[other, :, cut], part_in.at[at, :, cut], part_send.at[d, k], part_recv.at[at, k],
            device_id={"row": other}, device_id_type=MESH)

    for k in range(vchunks):
        dots = lax.dot_general(query[...], val[k * vstep:(k + 1) * vstep, :], contract,
                               preferred_element_type=jnp.float32)
        part[:, :, LANES + k * vstep:LANES + (k + 1) * vstep] = dots.reshape(R, group, vstep)
        loops(R, lambda d: part_copy(d, k, True).start())

    factor = float(rank)

    def own_sum(cut, k):
        if R <= 8:
            total = part[r, :, cut]
            for d in range(1, R):
                total = total + part_in[lax.rem(r + d, R), :, cut]
            return total
        return lax.fori_loop(1, R, lambda d, a: a + part_in[lax.rem(r + d, R), :, cut], part[r, :, cut])

    loops(R, lambda d: vsq_copy(d, False).wait_recv())
    if R <= 8:
        val_sq = vsq[...]
        for d in range(1, R):
            val_sq = val_sq + vsq_in[lax.rem(r + d, R)]
    else:
        val_sq = lax.fori_loop(1, R, lambda d, a: a + vsq_in[lax.rem(r + d, R)], vsq[...])
    val_scale = lax.rsqrt(val_sq + 1e-06)
    train_scale = None
    for k in range(vchunks):
        loops(R, lambda d: part_copy(d, k, False).wait_recv())
        if k == 0:
            train = jnp.sum(own_sum(slice(0, LANES), 0), axis=1, keepdims=True)
            train_scale = lax.rsqrt(train + 1e-06) * factor
        dots = own_sum(slice(LANES + k * vstep, LANES + (k + 1) * vstep), k)
        out_ref[:, k * vstep:(k + 1) * vstep] = (
            dots * train_scale * val_scale[:, k * vstep:(k + 1) * vstep])

    for copy in pairs:
        copy.wait_send()
    loops(R * C, lambda d: sketch_copy(d).wait_send())
    loops(R, lambda d: vsq_copy(d, True).wait_send())
    for k in range(vchunks):
        loops(R, lambda d: part_copy(d, k, True).wait_send())


def on_device(sizes, activations, out_grads, proj_in, proj_out, lengths, val_sketches):
    R, C, T = sizes
    tokens, ff = activations.shape
    width = out_grads.shape[1]
    rank = proj_in.shape[1]
    examples = lengths.shape[0]
    nv, own = val_sketches.shape
    group = C * examples
    chunks, vchunks = 4, 2
    bf16, f32 = jnp.bfloat16, jnp.float32
    tiles = rank // 2 // TILE
    scratch = [
        pltpu.VMEM((tokens, ff), bf16),
        pltpu.VMEM((tokens, width), bf16),
        pltpu.VMEM((rank, ff), bf16),
        pltpu.VMEM((2 * rank, width), bf16),
        pltpu.SMEM((examples,), jnp.int32),
        pltpu.VMEM((nv, own), bf16),
        pltpu.VMEM((rank + tokens, LANES), f32),
        pltpu.VMEM((T, rank + tokens, LANES), f32),
        pltpu.VMEM((examples, rank, LANES), f32),
        pltpu.VMEM((tiles, examples, TILE, LANES), bf16),
        pltpu.VMEM((R * C, examples, TILE, LANES), bf16),
        pltpu.VMEM((R * C, examples, TILE, LANES), f32),
        pltpu.VMEM((R * C * examples, own), bf16),
        pltpu.VMEM((nv, LANES), f32),
        pltpu.VMEM((1, nv), f32),
        pltpu.VMEM((R, 1, nv), f32),
        pltpu.VMEM((R, group, LANES + nv), f32),
        pltpu.VMEM((R, group, LANES + nv), f32),
        pltpu.SemaphoreType.DMA((chunks + 4, 2)),
        pltpu.SemaphoreType.DMA((vchunks,)),
        pltpu.SemaphoreType.DMA((T,)),
        pltpu.SemaphoreType.DMA((T,)),
        pltpu.SemaphoreType.DMA((R * C,)),
        pltpu.SemaphoreType.DMA((R * C,)),
        pltpu.SemaphoreType.DMA((R,)),
        pltpu.SemaphoreType.DMA((R,)),
        pltpu.SemaphoreType.DMA((R, vchunks)),
        pltpu.SemaphoreType.DMA((R, vchunks)),
    ]
    return pl.pallas_call(
        functools.partial(kernel, sizes),
        out_shape=jax.ShapeDtypeStruct((group, nv), f32),
        in_specs=[pl.BlockSpec(memory_space=pltpu.HBM)] * 6,
        out_specs=pl.BlockSpec(memory_space=pltpu.VMEM),
        scratch_shapes=scratch,
        compiler_params=pltpu.CompilerParams(
            collective_id=0, has_side_effects=True, vmem_limit_bytes=32 * 1024 * 1024
        ),
    )(*[pltpu.with_memory_space_constraint(x, pltpu.HBM) for x in
        (activations, out_grads, proj_in.T, proj_out.T, lengths, val_sketches)])


def solution(mesh):
    sizes = (mesh.shape["row"], mesh.shape["col"], mesh.shape["tensor"])
    placed = (
        P(("groups", "row", "col"), "tensor"),
        P(("groups", "row", "col"), "tensor"),
        P("tensor", None),
        P("tensor", None),
        P(("groups", "row", "col")),
        P(("groups", "col", "tensor"), "row"),
    )
    return jax.shard_map(
        functools.partial(on_device, sizes),
        mesh=mesh,
        in_specs=placed,
        out_specs=P(("groups", "row"), ("col", "tensor")),
        check_vma=False,
    )
```

```python
import functools

import jax
import jax.numpy as jnp
from jax import lax
from jax.experimental import pallas as pl
from jax.experimental.pallas import tpu as pltpu
from jax.sharding import PartitionSpec as P

MESH = pl.DeviceIdType.MESH
LANES = 128
TILE = 16


def columns(start, size):
    return pl.ds(start, size)


def kernel(sizes, act_hbm, grad_hbm, win_hbm, wout_hbm, len_hbm, val_hbm, out_ref,
           act, grad, win, wout, lens, val, half, half_in, wide, packed, landed, flat, query,
           squares, vsq, vsq_in, part, part_in,
           load_sem, val_sem, pair_send, pair_recv, sk_send, sk_recv, vsq_send, vsq_recv,
           part_send, part_recv):
    R, C, T = sizes
    r, c, t = lax.axis_index("row"), lax.axis_index("col"), lax.axis_index("tensor")
    me = r * C + c
    examples = lens.shape[0]
    slots = act.shape[0] // examples
    rank = win.shape[0]
    ff = act.shape[1]
    nv, own = val.shape
    group = C * examples
    groups = own // LANES
    chunks = load_sem.shape[0] - 4
    step = ff // chunks
    vchunks = val_sem.shape[0]
    vstep = nv // vchunks

    def loops(n, body):
        if n <= 8:
            for d in range(1, n):
                body(d)
        else:
            pl.loop(1, n)(body)

    barrier = pltpu.get_barrier_semaphore()

    def greet(d):
        other = lax.rem(me + d, R * C)
        pl.semaphore_signal(barrier, inc=1, device_id={"row": other // C, "col": lax.rem(other, C)},
                            device_id_type=MESH)

    loops(R * C, greet)
    for d in range(1, T):
        pl.semaphore_signal(barrier, inc=1, device_id={"tensor": lax.rem(t + d, T)}, device_id_type=MESH)

    loads = []
    for k in range(chunks):
        cut = columns(k * step, step)
        loads.append([
            pltpu.make_async_copy(act_hbm.at[:, cut], act.at[:, cut], load_sem.at[k, 0]),
            pltpu.make_async_copy(win_hbm.at[:, cut], win.at[:, cut], load_sem.at[k, 1]),
        ])
    tail = [
        pltpu.make_async_copy(grad_hbm, grad, load_sem.at[chunks, 0]),
        pltpu.make_async_copy(wout_hbm, wout.at[0:rank], load_sem.at[chunks + 1, 0]),
        pltpu.make_async_copy(wout_hbm, wout.at[rank:2 * rank], load_sem.at[chunks + 2, 0]),
        pltpu.make_async_copy(len_hbm, lens, load_sem.at[chunks + 3, 0]),
    ]
    vloads = [
        pltpu.make_async_copy(val_hbm.at[pl.ds(k * vstep, vstep)], val.at[pl.ds(k * vstep, vstep)],
                              val_sem.at[k])
        for k in range(vchunks)
    ]
    for copy in tail:
        copy.start()
    for pair in loads:
        for copy in pair:
            copy.start()

    contract = (((1,), (1,)), ((), ()))
    for copy in tail:
        copy.wait()
    half[rank:, :] = lax.dot_general(grad[...], wout[...], contract, preferred_element_type=jnp.float32)
    total = None
    for k in range(chunks):
        for copy in loads[k]:
            copy.wait()
        if k == chunks - 1:
            for copy in vloads:
                copy.start()
        cut = slice(k * step, (k + 1) * step)
        term = lax.dot_general(win[:, cut], act[:, cut], contract, preferred_element_type=jnp.float32)
        total = term if total is None else total + term
    half[0:rank, :] = total

    pl.semaphore_wait(barrier, R * C - 1 + T - 1)

    pairs = []
    for d in range(1, T):
        other = lax.rem(t + d, T)
        copy = pltpu.make_async_remote_copy(
            half, half_in.at[t], pair_send.at[d], pair_recv.at[t],
            device_id={"tensor": other}, device_id_type=MESH)
        copy.start()
        pairs.append(copy)

    def val_squares(k):
        vloads[k].wait()
        rows = 64
        for b in range(vstep // rows):
            base = k * vstep + b * rows
            acc = None
            for g in range(groups):
                x = val[base:base + rows, g * LANES:(g + 1) * LANES].astype(jnp.float32)
                acc = x * x if acc is None else acc + x * x
            squares[base:base + rows, :] = acc


    joined = half[...]
    for d in range(1, T):
        other = lax.rem(t + d, T)
        pltpu.make_async_remote_copy(
            half, half_in.at[other], pair_send.at[d], pair_recv.at[other],
            device_id={"tensor": other}, device_id_type=MESH).wait_recv()
        joined = joined + half_in[other]
    left_t = joined[0:rank].astype(jnp.bfloat16)
    right = joined[rank:].astype(jnp.bfloat16).astype(jnp.float32)
    slot = lax.broadcasted_iota(jnp.int32, right.shape, 0)
    blocks = []
    for e in range(examples):
        kept = (slot >= e * slots) & (slot < e * slots + lens[e])
        blocks.append(jnp.where(kept, right, 0.0).astype(jnp.bfloat16))
    wide_right = jnp.concatenate(blocks, axis=1)
    outer = jnp.dot(left_t, wide_right, preferred_element_type=jnp.float32)
    lane = lax.broadcasted_iota(jnp.int32, (rank // 2, LANES), 1)
    for e in range(examples):
        wide[e] = outer[:, e * LANES:(e + 1) * LANES]
    for e in range(examples):
        even = wide[e, pl.ds(0, rank // 2, stride=2), :]
        odd = wide[e, pl.ds(1, rank // 2, stride=2), :]
        sketch = jnp.where(lane < rank, even, odd).astype(jnp.bfloat16)
        for b in range(rank // 2 // TILE):
            packed[b, e] = sketch[b * TILE:(b + 1) * TILE]

    def tile_of(row):
        return (row * groups) // TILE

    def sketch_copy(d):
        other = lax.rem(me + d, R * C)
        return pltpu.make_async_remote_copy(
            packed.at[tile_of(other // C)], landed.at[me], sk_send.at[d], sk_recv.at[me],
            device_id={"row": other // C, "col": lax.rem(other, C)}, device_id_type=MESH)

    def sketch_arrival(d):
        other = lax.rem(me + d, R * C)
        return pltpu.make_async_remote_copy(
            packed.at[0], landed.at[other], sk_send.at[d], sk_recv.at[other],
            device_id={"row": other // C, "col": lax.rem(other, C)}, device_id_type=MESH)

    loops(R * C, lambda d: sketch_copy(d).start())

    for k in range(vchunks):
        val_squares(k)
    ones = jnp.ones((8, LANES), jnp.bfloat16)
    high = squares[...].astype(jnp.bfloat16)
    low = (squares[...] - high.astype(jnp.float32)).astype(jnp.bfloat16)
    sums = (lax.dot_general(ones, high, contract, preferred_element_type=jnp.float32)
            + lax.dot_general(ones, low, contract, preferred_element_type=jnp.float32))
    vsq[...] = sums[0:1]

    def vsq_copy(d, mine):
        other = lax.rem(r + d, R)
        at = r if mine else other
        return pltpu.make_async_remote_copy(
            vsq, vsq_in.at[at], vsq_send.at[d], vsq_recv.at[at],
            device_id={"row": other}, device_id_type=MESH)

    loops(R, lambda d: vsq_copy(d, True).start())

    flat[me] = packed[tile_of(r)].astype(jnp.float32)

    def take(d):
        other = lax.rem(me + d, R * C)
        sketch_arrival(d).wait_recv()
        flat[other] = landed[other].astype(jnp.float32)

    loops(R * C, take)

    offset = lax.rem(r * groups, TILE)
    rows = flat.reshape(R * C * examples * TILE, LANES)
    train_sq = jnp.zeros((R * C * examples, LANES), jnp.float32)
    for g in range(groups):
        piece = rows[pl.ds(offset + g, R * C * examples, stride=TILE), :]
        train_sq = train_sq + piece * piece
        query[:, g * LANES:(g + 1) * LANES] = piece.astype(jnp.bfloat16)
    part[:, :, 0:LANES] = train_sq.reshape(R, group, LANES)

    def part_copy(d, k, mine):
        other = lax.rem(r + d, R)
        at = r if mine else other
        cut = columns(0, LANES + vstep) if k == 0 else columns(LANES + k * vstep, vstep)
        return pltpu.make_async_remote_copy(
            part.at[other, :, cut], part_in.at[at, :, cut], part_send.at[d, k], part_recv.at[at, k],
            device_id={"row": other}, device_id_type=MESH)

    for k in range(vchunks):
        dots = lax.dot_general(query[...], val[k * vstep:(k + 1) * vstep, :], contract,
                               preferred_element_type=jnp.float32)
        part[:, :, LANES + k * vstep:LANES + (k + 1) * vstep] = dots.reshape(R, group, vstep)
        loops(R, lambda d: part_copy(d, k, True).start())

    factor = float(rank)

    def own_sum(cut, k):
        if R <= 8:
            total = part[r, :, cut]
            for d in range(1, R):
                total = total + part_in[lax.rem(r + d, R), :, cut]
            return total
        return lax.fori_loop(1, R, lambda d, a: a + part_in[lax.rem(r + d, R), :, cut], part[r, :, cut])

    loops(R, lambda d: vsq_copy(d, False).wait_recv())
    if R <= 8:
        val_sq = vsq[...]
        for d in range(1, R):
            val_sq = val_sq + vsq_in[lax.rem(r + d, R)]
    else:
        val_sq = lax.fori_loop(1, R, lambda d, a: a + vsq_in[lax.rem(r + d, R)], vsq[...])
    val_scale = lax.rsqrt(val_sq + 1e-06)
    train_scale = None
    for k in range(vchunks):
        loops(R, lambda d: part_copy(d, k, False).wait_recv())
        if k == 0:
            train = jnp.sum(own_sum(slice(0, LANES), 0), axis=1, keepdims=True)
            train_scale = lax.rsqrt(train + 1e-06) * factor
        dots = own_sum(slice(LANES + k * vstep, LANES + (k + 1) * vstep), k)
        out_ref[:, k * vstep:(k + 1) * vstep] = (
            dots * train_scale * val_scale[:, k * vstep:(k + 1) * vstep])

    for copy in pairs:
        copy.wait_send()
    loops(R * C, lambda d: sketch_copy(d).wait_send())
    loops(R, lambda d: vsq_copy(d, True).wait_send())
    for k in range(vchunks):
        loops(R, lambda d: part_copy(d, k, True).wait_send())


def on_device(sizes, activations, out_grads, proj_in, proj_out, lengths, val_sketches):
    R, C, T = sizes
    tokens, ff = activations.shape
    width = out_grads.shape[1]
    rank = proj_in.shape[1]
    examples = lengths.shape[0]
    nv, own = val_sketches.shape
    group = C * examples
    chunks, vchunks = 4, 1
    bf16, f32 = jnp.bfloat16, jnp.float32
    tiles = rank // 2 // TILE
    scratch = [
        pltpu.VMEM((tokens, ff), bf16),
        pltpu.VMEM((tokens, width), bf16),
        pltpu.VMEM((rank, ff), bf16),
        pltpu.VMEM((2 * rank, width), bf16),
        pltpu.SMEM((examples,), jnp.int32),
        pltpu.VMEM((nv, own), bf16),
        pltpu.VMEM((rank + tokens, LANES), f32),
        pltpu.VMEM((T, rank + tokens, LANES), f32),
        pltpu.VMEM((examples, rank, LANES), f32),
        pltpu.VMEM((tiles, examples, TILE, LANES), bf16),
        pltpu.VMEM((R * C, examples, TILE, LANES), bf16),
        pltpu.VMEM((R * C, examples, TILE, LANES), f32),
        pltpu.VMEM((R * C * examples, own), bf16),
        pltpu.VMEM((nv, LANES), f32),
        pltpu.VMEM((1, nv), f32),
        pltpu.VMEM((R, 1, nv), f32),
        pltpu.VMEM((R, group, LANES + nv), f32),
        pltpu.VMEM((R, group, LANES + nv), f32),
        pltpu.SemaphoreType.DMA((chunks + 4, 2)),
        pltpu.SemaphoreType.DMA((vchunks,)),
        pltpu.SemaphoreType.DMA((T,)),
        pltpu.SemaphoreType.DMA((T,)),
        pltpu.SemaphoreType.DMA((R * C,)),
        pltpu.SemaphoreType.DMA((R * C,)),
        pltpu.SemaphoreType.DMA((R,)),
        pltpu.SemaphoreType.DMA((R,)),
        pltpu.SemaphoreType.DMA((R, vchunks)),
        pltpu.SemaphoreType.DMA((R, vchunks)),
    ]
    return pl.pallas_call(
        functools.partial(kernel, sizes),
        out_shape=jax.ShapeDtypeStruct((group, nv), f32),
        in_specs=[pl.BlockSpec(memory_space=pltpu.HBM)] * 6,
        out_specs=pl.BlockSpec(memory_space=pltpu.VMEM),
        scratch_shapes=scratch,
        compiler_params=pltpu.CompilerParams(
            collective_id=0, has_side_effects=True, vmem_limit_bytes=32 * 1024 * 1024
        ),
    )(*[pltpu.with_memory_space_constraint(x, pltpu.HBM) for x in
        (activations, out_grads, proj_in.T, proj_out.T, lengths, val_sketches)])


def solution(mesh):
    sizes = (mesh.shape["row"], mesh.shape["col"], mesh.shape["tensor"])
    placed = (
        P(("groups", "row", "col"), "tensor"),
        P(("groups", "row", "col"), "tensor"),
        P("tensor", None),
        P("tensor", None),
        P(("groups", "row", "col")),
        P(("groups", "col", "tensor"), "row"),
    )
    return jax.shard_map(
        functools.partial(on_device, sizes),
        mesh=mesh,
        in_specs=placed,
        out_specs=P(("groups", "row"), ("col", "tensor")),
        check_vma=False,
    )
```
